32 devices in a mesh: seq: 8 (over z, x), head: 4 (over y, core).
Axes of the slice: x: 2, y: 2, z: 4, core: 2. Of those that a mesh axis runs over, the one named last changes fastest.
Arguments:
- query_rows: bfloat16 [8192, 4096], P('seq', 'head'), may hold values from -6 to 6
- key_rows: bfloat16 [8192, 4096], P('seq', 'head'), may hold values from -6 to 6
- value_rows: bfloat16 [8192, 4096], P('seq', 'head'), may hold values from -6 to 6
- out_grads: bfloat16 [8192, 4096], P(('seq', 'head')), may hold values from -6 to 6
Outputs:
- query_grad: bfloat16 [8192, 4096], P('seq', 'head')
- key_grad: bfloat16 [8192, 4096], P('seq', 'head')
- value_grad: bfloat16 [8192, 4096], P('seq', 'head')
The draws below stay inside these ranges and needn't reach their ends.
All inputs are finite; a program needn't handle non-finite values.
Results may differ from the reference program's by a relative error of at most 0.01.
Values may be sent and summed in bfloat16 or wider, within the bound.
No kernel may reach another device: no remote copies, remote signals or barrier semaphores. Data moves between devices by JAX's collectives and lax.ppermute only.
A program may use at most 128 MiB of HBM per device.

```python
import math
import jax
import jax.numpy as jnp
from jax import lax

D = 4096
HEADS = 32
HEAD_DIM = 128
GROUP = 512
TOKENS = 8192


def levels(rng, extent, shards, smallest, largest):
    level, own = 1.0, jax.random.fold_in(rng, 6)
    for dim, blocks in shards:
        draws = jnp.exp(jax.random.uniform(jax.random.fold_in(own, dim), (blocks,), jnp.float32, smallest / len(shards), largest / len(shards)))
        level = level * jnp.repeat(draws, extent[dim] // blocks).reshape([-1 if axis == dim else 1 for axis in range(len(extent))])
    return level


def gaussian(stream_key, shape, scale, most, cuts=(), dtype=jnp.bfloat16):
    values = scale * jax.random.normal(stream_key, shape, jnp.float32)
    if cuts:
        values = values * levels(stream_key, shape, cuts, -0.22, 0.18)
    return jnp.clip(values, -most, most).astype(dtype)


def setup_inputs(seed: int = 0) -> dict:
    keys = jax.random.split(jax.random.key(seed), 5)
    return {
        "query_rows": gaussian(keys[0], (TOKENS, D), 1.0, 6.0, ((0, 8), (1, 4))),
        "key_rows": gaussian(keys[1], (TOKENS, D), 1.0, 6.0, ((0, 8), (1, 4))),
        "value_rows": gaussian(keys[2], (TOKENS, D), 1.0, 6.0, ((0, 8), (1, 4))),
        "out_grads": gaussian(keys[3], (TOKENS, D), 1.0, 6.0, ((0, 32),)),
    }


def reference(query_rows, key_rows, value_rows, out_grads):
    blocks = TOKENS // GROUP
    factor = 1.0 / math.sqrt(HEAD_DIM * TOKENS)

    def split(array):
        return array.reshape(blocks, GROUP, HEADS, HEAD_DIM)
    queries, keyset, valueset, grads = (split(query_rows), split(key_rows), split(value_rows), split(out_grads))

    def block_states(items):
        key_blk, val_blk, qry_blk, grd_blk = items
        kv_state = jnp.einsum('thi,thj->hij', key_blk.astype(jnp.float32), val_blk.astype(jnp.float32)).astype(jnp.bfloat16)
        grad_state = jnp.einsum('thi,thj->hij', qry_blk.astype(jnp.float32), grd_blk.astype(jnp.float32)).astype(jnp.bfloat16)
        return (kv_state, grad_state)
    kv_state, grad_state = lax.map(block_states, (keyset, valueset, queries, grads))
    zero_state = jnp.zeros((1, HEADS, HEAD_DIM, HEAD_DIM), jnp.float32)
    prefix = jnp.concatenate([zero_state, jnp.cumsum(kv_state.astype(jnp.float32), axis=0)[:-1]], axis=0)
    flipped = jnp.cumsum(grad_state.astype(jnp.float32)[::-1], axis=0)[:-1]
    suffix = jnp.concatenate([flipped, zero_state], axis=0)[::-1]
    suffix = jnp.concatenate([jnp.cumsum(grad_state.astype(jnp.float32)[::-1], axis=0)[::-1][1:], zero_state], axis=0)
    prefix_low = prefix.astype(jnp.bfloat16)
    suffix_low = suffix.astype(jnp.bfloat16)
    causal = jnp.tril(jnp.ones((GROUP, GROUP), jnp.bool_))

    def block_grads(items):
        qry_blk, key_blk, val_blk, grd_blk, pre_blk, suf_blk = items
        qry_f = qry_blk.astype(jnp.float32)
        key_f = key_blk.astype(jnp.float32)
        val_f = val_blk.astype(jnp.float32)
        grd_f = grd_blk.astype(jnp.float32)
        fwd_scores = jnp.where(causal[None], factor * jnp.einsum('thi,shi->hts', qry_f, key_f), 0.0).astype(jnp.bfloat16).astype(jnp.float32)
        back_scores = jnp.where(causal[None], factor * jnp.einsum('thj,shj->hts', grd_f, val_f), 0.0).astype(jnp.bfloat16).astype(jnp.float32)
        pre_f = pre_blk.astype(jnp.float32)
        suf_f = suf_blk.astype(jnp.float32)
        qgrad = jnp.einsum('hts,shi->thi', back_scores, key_f) + factor * jnp.einsum('thj,hij->thi', grd_f, pre_f)
        kgrad = jnp.einsum('hts,thi->shi', back_scores, qry_f) + factor * jnp.einsum('shj,hij->shi', val_f, suf_f)
        vgrad = jnp.einsum('hts,thj->shj', fwd_scores, grd_f) + factor * jnp.einsum('shi,hij->shj', key_f, suf_f)
        return (qgrad.reshape(GROUP, D).astype(jnp.bfloat16), kgrad.reshape(GROUP, D).astype(jnp.bfloat16), vgrad.reshape(GROUP, D).astype(jnp.bfloat16))
    query_grad, key_grad, value_grad = lax.map(block_grads, (queries, keyset, valueset, grads, prefix_low, suffix_low))
    return (query_grad.reshape(TOKENS, D), key_grad.reshape(TOKENS, D), value_grad.reshape(TOKENS, D))
```

```python
import functools
import math

import jax
import jax.numpy as jnp
from jax import lax
from jax.experimental import pallas as pl
from jax.experimental.pallas import tpu as pltpu
from jax.sharding import PartitionSpec as P

HEAD_DIM = 128
SPLITS = (4, 2, 2)
F32 = jnp.float32
BF16 = jnp.bfloat16
NN = (((1,), (0,)), ((), ()))
NT = (((1,), (1,)), ((), ()))
TN = (((0,), (0,)), ((), ()))


def dot(a, b, dims):
    return lax.dot_general(a, b, dims, preferred_element_type=F32)


def params(**kw):
    return pltpu.CompilerParams(vmem_limit_bytes=48 * 1024 * 1024, **kw)


def cost(flops, bytes_accessed):
    return pl.CostEstimate(flops=int(flops), bytes_accessed=int(bytes_accessed), transcendentals=0)


def head_cols(h):
    return slice(h * HEAD_DIM, (h + 1) * HEAD_DIM)


def kv_kernel(heads, chunk, k_ref, v_ref, local_ref, total_ref):
    chunks = k_ref.shape[0] // chunk
    for h in range(heads):
        run = jnp.zeros((HEAD_DIM, HEAD_DIM), F32)
        for c in range(chunks):
            rows = slice(c * chunk, (c + 1) * chunk)
            local_ref[c, h] = run.astype(BF16)
            run = run + dot(v_ref[rows, head_cols(h)], k_ref[rows, head_cols(h)], TN)
        total_ref[h] = run.astype(BF16)


def kv_states(key_rows, value_rows, chunk, heads=4):
    rows, width = key_rows.shape
    head_count = width // HEAD_DIM
    chunks = rows // chunk
    spec = pl.BlockSpec((rows, heads * HEAD_DIM), lambda i: (0, i))
    return pl.pallas_call(
        functools.partial(kv_kernel, heads, chunk),
        grid=(head_count // heads,),
        in_specs=[spec, spec],
        out_specs=[
            pl.BlockSpec((chunks, heads, HEAD_DIM, HEAD_DIM), lambda i: (0, i, 0, 0)),
            pl.BlockSpec((heads, HEAD_DIM, HEAD_DIM), lambda i: (i, 0, 0)),
        ],
        out_shape=[
            jax.ShapeDtypeStruct((chunks, head_count, HEAD_DIM, HEAD_DIM), BF16),
            jax.ShapeDtypeStruct((head_count, HEAD_DIM, HEAD_DIM), BF16),
        ],
        compiler_params=params(),
        cost_estimate=cost(2 * rows * width * HEAD_DIM, 4 * rows * width),
        name="kv_states",
    )(key_rows, value_rows)


def intra_kernel(heads, with_state, place_ref, *refs):
    ins, outs = refs[:8], refs[8:]
    size = ins[0].shape[0]
    row = lax.broadcasted_iota(jnp.int32, (size, size), 0)
    col = lax.broadcasted_iota(jnp.int32, (size, size), 1)
    keep = row <= col
    for piece in range(2):
        q_ref, k_ref, v_ref, g_ref = ins[4 * piece : 4 * piece + 4]
        for h in range(heads):
            cols = head_cols(h)
            q, k, v, g = q_ref[:, cols], k_ref[:, cols], v_ref[:, cols], g_ref[:, cols]
            fwd = jnp.where(keep, dot(k, q, NT), 0.0).astype(BF16)
            back = jnp.where(keep, dot(v, g, NT), 0.0).astype(BF16)
            outs[0][piece, :, cols] = dot(back, k, TN).astype(outs[0].dtype)
            outs[1][piece, :, cols] = dot(back, q, NN).astype(outs[1].dtype)
            outs[2][piece, :, cols] = dot(fwd, g, NN).astype(outs[2].dtype)
            if with_state:
                outs[3][piece, h] = dot(q, g, TN).astype(BF16)


def intra(place, piece0, arrays, grads, first_own, head0, head_count, chunk, with_state, heads):
    width = heads * HEAD_DIM
    base = head0 // heads
    full = arrays[0].shape[1] // width

    def rows_spec(piece):
        return pl.BlockSpec((chunk, width), lambda i, place: (place[piece], i + base))

    def grad_spec(own):
        if own:
            return pl.BlockSpec((chunk, width), lambda i, place: (0, place[0] * full + i))
        return pl.BlockSpec((chunk, width), lambda i, place: (0, i))

    in_specs, operands = [], []
    for j in range(2):
        in_specs += [rows_spec(piece0 + j)] * 3 + [grad_spec(first_own and j == 0)]
        operands += list(arrays) + [grads[j]]
    out_specs = [pl.BlockSpec((2, chunk, width), lambda i, place: (0, 0, i))] * 3
    out_shape = [jax.ShapeDtypeStruct((2, chunk, head_count * HEAD_DIM), BF16)] * 3
    if with_state:
        out_specs.append(pl.BlockSpec((2, heads, HEAD_DIM, HEAD_DIM), lambda i, place: (0, i, 0, 0)))
        out_shape.append(jax.ShapeDtypeStruct((2, head_count, HEAD_DIM, HEAD_DIM), BF16))
    return pl.pallas_call(
        functools.partial(intra_kernel, heads, with_state),
        grid_spec=pltpu.PrefetchScalarGridSpec(
            num_scalar_prefetch=1,
            grid=(head_count // heads,),
            in_specs=in_specs,
            out_specs=out_specs,
        ),
        out_shape=out_shape,
        compiler_params=params(),
        cost_estimate=cost(
            2 * head_count * 10 * chunk * chunk * HEAD_DIM, 2 * 14 * chunk * head_count * HEAD_DIM
        ),
        name="intra",
    )(place, *operands)


def grad_state_kernel(heads, place_ref, q0, q1, g0, g1, near_ref, state_ref, total_ref):
    for h in range(heads):
        cols = head_cols(h)
        a = dot(q0[:, cols], g0[:, cols], TN)
        b = dot(q1[:, cols], g1[:, cols], TN)
        state_ref[0, h] = a.astype(BF16)
        state_ref[1, h] = b.astype(BF16)
        total = a + b + near_ref[0, h].astype(F32) + near_ref[1, h].astype(F32)
        total_ref[h] = total.astype(BF16)


def grad_states(place, query_rows, grads, near, head0, head_count, chunk):
    width = head_count * HEAD_DIM
    block = head0 // head_count

    def rows_spec(piece):
        return pl.BlockSpec((chunk, width), lambda i, place: (place[piece], block))

    whole = pl.BlockSpec((chunk, width), lambda i, place: (0, 0))
    return pl.pallas_call(
        functools.partial(grad_state_kernel, head_count),
        grid_spec=pltpu.PrefetchScalarGridSpec(
            num_scalar_prefetch=1,
            grid=(1,),
            in_specs=[
                rows_spec(2),
                rows_spec(3),
                whole,
                whole,
                pl.BlockSpec((2, head_count, HEAD_DIM, HEAD_DIM), lambda i, place: (0, block, 0, 0)),
            ],
            out_specs=[
                pl.BlockSpec((2, head_count, HEAD_DIM, HEAD_DIM), lambda i, place: (0, 0, 0, 0)),
                pl.BlockSpec((head_count, HEAD_DIM, HEAD_DIM), lambda i, place: (0, 0, 0)),
            ],
        ),
        out_shape=[
            jax.ShapeDtypeStruct((2, head_count, HEAD_DIM, HEAD_DIM), BF16),
            jax.ShapeDtypeStruct((head_count, HEAD_DIM, HEAD_DIM), BF16),
        ],
        compiler_params=params(),
        cost_estimate=cost(4 * chunk * width * HEAD_DIM, 8 * chunk * width),
        name="grad_states",
    )(place, query_rows, query_rows, *grads, near)


def finish_kernel(chunk, factor, rounds, aliased, place_ref, *refs):
    refs = list(refs)
    if aliased:
        refs = refs[3:]
    k_ref, v_ref = refs[:2]
    g_refs = refs[2:6]
    near = refs[6:9]
    far = refs[9:12]
    near_state, far_state, local_ref = refs[12:15]
    kv_in = refs[15 : 15 + rounds]
    grad_in = refs[15 + rounds : 15 + 2 * rounds]
    dq_ref, dk_ref, dv_ref = refs[15 + 2 * rounds :]
    odd = place_ref[4].astype(F32)
    prefix = kv_in[0][0].astype(F32) * odd
    suffix = grad_in[0][0].astype(F32) * (1.0 - odd)
    for r in range(1, rounds):
        prefix = prefix + kv_in[r][0].astype(F32)
        suffix = suffix + grad_in[r][0].astype(F32)
    states = [near_state[0, 0], near_state[1, 0], far_state[0, 0], far_state[1, 0]]
    states = [s.astype(F32) for s in states]
    for piece in range(4):
        place = place_ref[piece]
        rows = pl.ds(pl.multiple_of(place * chunk, chunk), chunk)
        part = near if piece < 2 else far
        prefix_low = (prefix + local_ref[place, 0].astype(F32)).astype(BF16)
        after = suffix
        for other in range(4):
            if other != piece:
                later = (place_ref[other] > place).astype(F32)
                after = after + later * states[other]
        after_low = after.astype(BF16)
        out = part[0][piece % 2].astype(F32) + dot(g_refs[piece][...], prefix_low, NN)
        dq_ref[rows, :] = (factor * out).astype(BF16)
        out = part[1][piece % 2].astype(F32) + dot(v_ref[rows, :], after_low, NT)
        dk_ref[rows, :] = (factor * out).astype(BF16)
        out = part[2][piece % 2].astype(F32) + dot(k_ref[rows, :], after_low, NN)
        dv_ref[rows, :] = (factor * out).astype(BF16)


def finish(
    place, key_rows, value_rows, grads, near, far, near_state, far_state, local, kv_in, grad_in,
    head0, head_count, chunk, factor, outs,
):
    rows, feat = key_rows.shape
    full = feat // HEAD_DIM
    rounds = len(kv_in)
    wide = pl.BlockSpec((rows, HEAD_DIM), lambda i, place: (0, i + head0))

    def piece_spec(shift):
        return pl.BlockSpec((chunk, HEAD_DIM), lambda i, place: (0, i + shift))

    def pair_spec(shift):
        return pl.BlockSpec((2, chunk, HEAD_DIM), lambda i, place: (0, 0, i + shift))

    def states_spec(count, shift):
        return pl.BlockSpec(
            (count, 1, HEAD_DIM, HEAD_DIM), lambda i, place: (0, i + shift, 0, 0)
        )

    def state_spec(shift):
        return pl.BlockSpec((1, HEAD_DIM, HEAD_DIM), lambda i, place: (i + shift, 0, 0))

    own = pl.BlockSpec((chunk, HEAD_DIM), lambda i, place: (0, place[0] * full + i + head0))
    in_specs = [wide, wide, own, piece_spec(head0), piece_spec(0), piece_spec(0)]
    in_specs += [pair_spec(head0)] * 3 + [pair_spec(0)] * 3
    in_specs += [states_spec(2, head0), states_spec(2, 0), states_spec(local.shape[0], head0)]
    in_specs += [state_spec(head0)] * rounds + [state_spec(0)] * rounds
    operands = [key_rows, value_rows, *grads, *near, *far, near_state, far_state, local]
    operands += [*kv_in, *grad_in]
    aliases = {}
    if outs is not None:
        in_specs = [pl.BlockSpec(memory_space=pl.ANY)] * 3 + in_specs
        operands = list(outs) + operands
        aliases = {1: 0, 2: 1, 3: 2}
    return pl.pallas_call(
        functools.partial(finish_kernel, chunk, factor, rounds, outs is not None),
        grid_spec=pltpu.PrefetchScalarGridSpec(
            num_scalar_prefetch=1,
            grid=(head_count,),
            in_specs=in_specs,
            out_specs=[wide] * 3,
        ),
        out_shape=[jax.ShapeDtypeStruct((rows, feat), BF16)] * 3,
        input_output_aliases=aliases,
        compiler_params=params(),
        cost_estimate=cost(
            6 * rows * head_count * HEAD_DIM * HEAD_DIM, 18 * rows * head_count * HEAD_DIM
        ),
        name="finish",
    )(place, *operands)


def seq_sums(total, axis, size, sign):
    other = lax.ppermute(total, axis, [(i, i ^ 1) for i in range(size)])
    parts = [other]
    window = total + other
    step = 2
    while step < size:
        pairs = [(i, i + sign * step) for i in range(size) if 0 <= i + sign * step < size]
        got = lax.ppermute(window, axis, pairs)
        parts.append(got)
        step *= 2
        if step < size:
            window = window + got
    return parts


def body(seq_size, head_size, query_rows, key_rows, value_rows, out_grads):
    rows, feat = query_rows.shape
    chunk = rows // head_size
    head_count = feat // HEAD_DIM
    factor = 1.0 / math.sqrt(HEAD_DIM * rows * seq_size)
    rank = lax.axis_index("head")
    odd = lax.axis_index("seq") % 2
    place = jnp.stack([rank, rank ^ 1, rank ^ 2, rank ^ 3, odd]).astype(jnp.int32)

    def exchange(mask, head0, heads):
        start = (rank ^ mask) * feat + head0 * HEAD_DIM
        block = lax.dynamic_slice(out_grads, (0, start), (chunk, heads * HEAD_DIM))
        return lax.ppermute(block, "head", [(i, i ^ mask) for i in range(head_size)])

    arrays = (query_rows, key_rows, value_rows)
    firsts = [sum(SPLITS[:s]) for s in range(len(SPLITS))]
    crossing = [[exchange(2, f, n), exchange(3, f, n)] for f, n in zip(firsts, SPLITS)]
    near_grad = exchange(1, 0, head_count)

    local, kv_total = kv_states(key_rows, value_rows, chunk)
    kv_in = seq_sums(kv_total, "seq", seq_size, 1)
    *near, near_state = intra(
        place, 0, arrays, (out_grads, near_grad), True, 0, head_count, chunk, True, 4
    )
    outs = None
    for f, n, grads in zip(firsts, SPLITS, crossing):
        far_state, total = grad_states(place, query_rows, grads, near_state, f, n, chunk)
        grad_in = seq_sums(total, "seq", seq_size, -1)
        far = intra(place, 2, arrays, grads, False, f, n, chunk, False, 2)
        outs = finish(
            place, key_rows, value_rows, (out_grads, near_grad, *grads), near, far, near_state,
            far_state, local, kv_in, grad_in, f, n, chunk, factor, outs,
        )
    return tuple(outs)


def solution(mesh):
    return jax.shard_map(
        functools.partial(body, mesh.shape["seq"], mesh.shape["head"]),
        mesh=mesh,
        in_specs=(P("seq", "head"), P("seq", "head"), P("seq", "head"), P(("seq", "head"), None)),
        out_specs=(P("seq", "head"), P("seq", "head"), P("seq", "head")),
        check_vma=False,
    )
```

```python
import functools
import math

import jax
import jax.numpy as jnp
from jax import lax
from jax.experimental import pallas as pl
from jax.experimental.pallas import tpu as pltpu
from jax.sharding import PartitionSpec as P

HEAD_DIM = 128
SPLITS = (4, 4)
COST = (10**10, 10**8)
F32 = jnp.float32
BF16 = jnp.bfloat16
NN = (((1,), (0,)), ((), ()))
NT = (((1,), (1,)), ((), ()))
TN = (((0,), (0,)), ((), ()))
VMEM = pl.BlockSpec(memory_space=pltpu.VMEM)
ANY = pl.BlockSpec(memory_space=pl.ANY)


def dot(a, b, dims):
    return lax.dot_general(a, b, dims, preferred_element_type=F32)


def head_cols(h):
    return slice(h * HEAD_DIM, (h + 1) * HEAD_DIM)


def rows_of(place_ref, piece, chunk):
    return pl.ds(pl.multiple_of(place_ref[piece] * chunk, chunk), chunk)


def place_as(array, spec):
    return pltpu.with_memory_space_constraint(array, pltpu.VMEM if spec is VMEM else pltpu.HBM)


class Chain:
    def __init__(self, place):
        self.place = place
        self.token = jnp.zeros((8, 128), F32) + place[0].astype(F32)
        self.waits = []
        self.jobs = []

    def add(self, *sums):
        self.jobs += [one for one in sums if one.more()]

    def wait(self, *arrays):
        self.waits += arrays

    def __call__(self, name, kernel, operands, in_specs, out_shape, out_specs, grid=(), scratch=(), alias=None, cost=COST):
        extra = [self.token, *self.waits]
        jobs, self.waits, self.jobs = self.jobs, [], []
        skip, count = len(extra), len(operands)
        pairs = [array for sums in jobs for array in (sums.window, sums.parts[-1])]
        operands, in_specs = [*operands, *pairs], [*in_specs, *[VMEM] * len(pairs)]
        out_shape = [*[bf16(*sums.window.shape) for sums in jobs], *out_shape]
        out_specs = [*[VMEM] * len(jobs), *out_specs]

        def run(place_ref, *refs):
            ins = refs[skip : skip + count]
            pair_refs = refs[skip + count : skip + len(operands)]
            outs = refs[skip + len(operands) + 1 :]
            for n in range(len(jobs)):
                outs[n][...] = pair_refs[2 * n][...] + pair_refs[2 * n + 1][...]
            kernel(place_ref, *ins, *outs[len(jobs) :])

        aliases = {1: 0}
        for source, target in (alias or {}).items():
            aliases[1 + skip + source] = 1 + len(jobs) + target
        self.token, *outs = pl.pallas_call(
            run,
            grid_spec=pltpu.PrefetchScalarGridSpec(
                num_scalar_prefetch=1,
                grid=grid,
                in_specs=[ANY] * skip + list(in_specs),
                out_specs=[ANY] + list(out_specs),
                scratch_shapes=list(scratch),
            ),
            out_shape=[jax.ShapeDtypeStruct((8, 128), F32)] + list(out_shape),
            input_output_aliases=aliases,
            compiler_params=pltpu.CompilerParams(vmem_limit_bytes=8 * 1024 * 1024),
            cost_estimate=pl.CostEstimate(flops=cost[0], bytes_accessed=cost[1], transcendentals=0),
            name=name,
        )(self.place, *extra, *[place_as(x, s) for x, s in zip(operands, in_specs)])
        for sums, window in zip(jobs, outs):
            sums.window = window
            sums.go()
        return outs[len(jobs) :]


def bf16(*shape):
    return pltpu.VMEM(shape, BF16)


def cut(chain, out_grads, parts):
    chunk = out_grads.shape[0]

    def kernel(place_ref, g_ref, *refs):
        outs, sems = refs[:-1], refs[-1]
        copies = []
        for n, (mask, head0, heads) in enumerate(parts):
            start = place_ref[mask] * place_ref[4] + head0 * HEAD_DIM
            cols = pl.ds(pl.multiple_of(start, HEAD_DIM), heads * HEAD_DIM)
            copies.append(pltpu.make_async_copy(g_ref.at[:, cols], outs[n], sems.at[n]))
        for copy in copies:
            copy.start()
        for copy in copies:
            copy.wait()

    return chain(
        "cut", kernel, [out_grads], [ANY],
        [bf16(chunk, heads * HEAD_DIM) for _, _, heads in parts], [VMEM] * len(parts),
        scratch=[pltpu.SemaphoreType.DMA((len(parts),))],
    )


def kv_states(chain, key_rows, value_rows, chunk):
    rows, width = key_rows.shape
    heads, chunks = width // HEAD_DIM, rows // chunk

    def kernel(place_ref, k_ref, v_ref, local_ref, total_ref):
        for h in range(heads):
            run = jnp.zeros((HEAD_DIM, HEAD_DIM), F32)
            for c in range(chunks):
                at = slice(c * chunk, (c + 1) * chunk)
                local_ref[c, h] = run.astype(BF16)
                run = run + dot(v_ref[at, head_cols(h)], k_ref[at, head_cols(h)], TN)
            total_ref[h] = run.astype(BF16)

    return chain(
        "kv_states", kernel, [key_rows, value_rows], [VMEM] * 2,
        [bf16(chunks, heads, HEAD_DIM, HEAD_DIM), bf16(heads, HEAD_DIM, HEAD_DIM)], [VMEM] * 2,
    )


def intra(chain, pieces, arrays, grads, head0, heads, chunk):
    count = len(pieces)

    def kernel(place_ref, q_ref, k_ref, v_ref, *refs):
        g_refs, outs = refs[:count], refs[count:]
        row = lax.broadcasted_iota(jnp.int32, (chunk, chunk), 0)
        col = lax.broadcasted_iota(jnp.int32, (chunk, chunk), 1)
        upper, lower = row <= col, row >= col
        for n, piece in enumerate(pieces):
            rows = rows_of(place_ref, piece, chunk)
            for h in range(heads):
                cols, own = head_cols(head0 + h), head_cols(h)
                q, k, v, g = q_ref[rows, cols], k_ref[rows, cols], v_ref[rows, cols], g_refs[n][:, own]
                fwd = jnp.where(upper, dot(k, q, NT), 0.0).astype(BF16)
                back = jnp.where(upper, dot(v, g, NT), 0.0).astype(BF16)
                turned = jnp.where(lower, dot(g, v, NT), 0.0).astype(BF16)
                outs[0][n, :, own] = dot(turned, k, NN).astype(BF16)
                outs[1][n, :, own] = dot(back, q, NN).astype(BF16)
                outs[2][n, :, own] = dot(fwd, g, NN).astype(BF16)

    shapes = [bf16(count, chunk, heads * HEAD_DIM)] * 3
    return chain(
        "intra", kernel, [*arrays, *grads], [VMEM] * (3 + count), shapes, [VMEM] * len(shapes)
    )


def near_states(chain, query_rows, grads, chunk):
    heads = query_rows.shape[1] // HEAD_DIM

    def kernel(place_ref, q_ref, g0, g1, state_ref):
        for h in range(heads):
            cols = head_cols(h)
            for n, g_ref in enumerate((g0, g1)):
                q = q_ref[rows_of(place_ref, n, chunk), cols]
                state_ref[n, h] = dot(q, g_ref[:, cols], TN).astype(BF16)

    return chain(
        "near_states", kernel, [query_rows, *grads], [VMEM] * 3,
        [bf16(2, heads, HEAD_DIM, HEAD_DIM)], [VMEM],
    )[0]


def far_states(chain, query_rows, grads, near, head0, heads, chunk):
    def kernel(place_ref, q_ref, g0, g1, near_ref, state_ref, total_ref):
        for h in range(heads):
            cols, own = head_cols(head0 + h), head_cols(h)
            a = dot(q_ref[rows_of(place_ref, 2, chunk), cols], g0[:, own], TN)
            b = dot(q_ref[rows_of(place_ref, 3, chunk), cols], g1[:, own], TN)
            state_ref[0, h] = a.astype(BF16)
            state_ref[1, h] = b.astype(BF16)
            total = a + b + near_ref[0, head0 + h].astype(F32) + near_ref[1, head0 + h].astype(F32)
            total_ref[h] = total.astype(BF16)

    return chain(
        "far_states", kernel, [query_rows, *grads, near], [VMEM] * 4,
        [bf16(2, heads, HEAD_DIM, HEAD_DIM), bf16(heads, HEAD_DIM, HEAD_DIM)], [VMEM] * 2,
    )


def finish(chain, key_rows, value_rows, grads, parts, states, local, kv_in, grad_in, last, head0, heads, chunk, factor, outs):
    rows, feat = key_rows.shape
    rounds = len(kv_in)

    def kernel(place_ref, *refs):
        refs = list(refs)
        if outs is not None:
            refs = refs[3:]

        def take(n):
            got = refs[:n]
            del refs[:n]
            return got

        k_ref, v_ref = take(2)
        g_refs = take(4)
        part_refs = [take(3), take(3), take(3)]
        state_refs = take(2)
        (local_ref,) = take(1)
        kv_refs, grad_refs = take(rounds), take(rounds)
        (last_ref,) = take(1)
        dq_ref, dk_ref, dv_ref = refs
        h = pl.program_id(0)
        bit = place_ref[5 + rounds].astype(F32)
        got = last_ref[h].astype(F32)
        prefix, suffix = got * bit, got * (1.0 - bit)
        for r in range(rounds):
            bit = place_ref[5 + r].astype(F32)
            prefix = prefix + kv_refs[r][head0 + h].astype(F32) * bit
            suffix = suffix + grad_refs[r][h].astype(F32) * (1.0 - bit)
        wide = pl.ds(pl.multiple_of((head0 + h) * HEAD_DIM, HEAD_DIM), HEAD_DIM)
        narrow = pl.ds(pl.multiple_of(h * HEAD_DIM, HEAD_DIM), HEAD_DIM)
        state = [
            state_refs[0][0, head0 + h], state_refs[0][1, head0 + h],
            state_refs[1][0, h], state_refs[1][1, h],
        ]
        state = [s.astype(F32) for s in state]
        for piece in range(4):
            place = place_ref[piece]
            at = rows_of(place_ref, piece, chunk)
            part, slot = part_refs[min(piece, 2)], max(piece - 2, 0)
            cols = wide if piece < 2 else narrow
            before_low = (prefix + local_ref[place, head0 + h].astype(F32)).astype(BF16)
            after = suffix
            for other in range(4):
                if other != piece:
                    later = (place_ref[other] > place).astype(F32)
                    after = after + later * state[other]
            after_low = after.astype(BF16)
            out = part[0][slot, :, cols].astype(F32) + dot(g_refs[piece][:, cols], before_low, NN)
            dq_ref[at, :] = (factor * out).astype(BF16)
            out = part[1][slot, :, cols].astype(F32) + dot(v_ref[at, wide], after_low, NT)
            dk_ref[at, :] = (factor * out).astype(BF16)
            out = part[2][slot, :, cols].astype(F32) + dot(k_ref[at, wide], after_low, NN)
            dv_ref[at, :] = (factor * out).astype(BF16)

    operands = [key_rows, value_rows, *grads]
    for p in parts:
        operands += p
    operands += [*states, local, *kv_in, *grad_in, last]
    in_specs = [VMEM] * len(operands)
    alias = {}
    if outs is not None:
        operands = [*outs, *operands]
        in_specs = [ANY] * 3 + in_specs
        alias = {0: 0, 1: 1, 2: 2}
    return chain(
        "finish", kernel, operands, in_specs, [pltpu.HBM((rows, feat), BF16)] * 3,
        [pl.BlockSpec((rows, HEAD_DIM), lambda i, place: (0, i + head0))] * 3,
        grid=(heads,), alias=alias,
    )


class SeqSums:
    def __init__(self, total, axis, size):
        self.window, self.axis, self.size = total, axis, size
        self.step, self.parts = 1, []

    def swap(self, block):
        got = lax.ppermute(block, self.axis, [(i, i ^ self.step) for i in range(self.size)])
        self.step *= 2
        return got

    def more(self):
        return 2 * self.step < self.size

    def go(self):
        self.parts.append(self.swap(self.window))


def add_only(chain):
    if chain.jobs:
        chain("add", lambda place_ref: None, [], [], [], [])


def last_round(chain, prefix_sums, suffix_sums, head0, heads):
    rounds = len(suffix_sums.parts)

    def kernel(place_ref, kv_a, kv_b, grad_a, grad_b, out_ref):
        upper = place_ref[5 + rounds] == 1

        @pl.when(upper)
        def _():
            out_ref[...] = grad_a[...] + grad_b[...]

        @pl.when(jnp.logical_not(upper))
        def _():
            at = slice(head0, head0 + heads)
            out_ref[...] = kv_a[at] + kv_b[at]

    operands = [prefix_sums.window, prefix_sums.parts[-1], suffix_sums.window, suffix_sums.parts[-1]]
    block = chain("last_round", kernel, operands, [VMEM] * 4, [bf16(heads, HEAD_DIM, HEAD_DIM)], [VMEM])[0]
    return suffix_sums.swap(block)


def body(seq_size, head_size, query_rows, key_rows, value_rows, out_grads):
    rows, feat = query_rows.shape
    chunk = rows // head_size
    head_count = feat // HEAD_DIM
    factor = 1.0 / math.sqrt(HEAD_DIM * rows * seq_size)
    rank = lax.axis_index("head")
    seq = lax.axis_index("seq")
    bits = [(seq >> r) & 1 for r in range(seq_size.bit_length() - 1)]
    place = jnp.stack([rank, rank ^ 1, rank ^ 2, rank ^ 3, jnp.full_like(rank, feat), *bits])
    chain = Chain(place.astype(jnp.int32))
    arrays = (query_rows, key_rows, value_rows)
    firsts = [sum(SPLITS[:s]) for s in range(len(SPLITS))]

    def send(block, mask):
        return lax.ppermute(block, "head", [(i, i ^ mask) for i in range(head_size)])

    f, n = firsts[0], SPLITS[0]
    near_block, *blocks = cut(chain, out_grads, [(1, 0, head_count), (2, f, n), (3, f, n)])
    near_grad = send(near_block, 1)
    crossing = [[send(blocks[0], 2), send(blocks[1], 3)]]
    local, kv_total = kv_states(chain, key_rows, value_rows, chunk)
    kv_sums = SeqSums(kv_total, "seq", seq_size)
    kv_sums.go()
    chain.wait(near_grad)
    f, n = firsts[1], SPLITS[1]
    own_grad, *blocks = cut(chain, out_grads, [(0, 0, head_count), (2, f, n), (3, f, n)])
    crossing.append([send(blocks[0], 2), send(blocks[1], 3)])
    own_part = intra(chain, [0], arrays, [own_grad], 0, head_count, chunk)
    near_state = near_states(chain, query_rows, (own_grad, near_grad), chunk)
    near_part = intra(chain, [1], arrays, [near_grad], 0, head_count, chunk)

    far_state, far_part, sums, lasts = [], [], [], []

    def states(s):
        f, n = firsts[s], SPLITS[s]
        far, total = far_states(chain, query_rows, crossing[s], near_state, f, n, chunk)
        far_state.append(far)
        sums.append(SeqSums(total, "seq", seq_size))
        sums[s].go()

    def settle(one):
        while one.more():
            chain.add(one)
            add_only(chain)

    def inside(s):
        far_part.append(intra(chain, [2, 3], arrays, crossing[s], firsts[s], SPLITS[s], chunk))

    def last(s):
        settle(sums[s])
        lasts.append(last_round(chain, kv_sums, sums[s], firsts[s], SPLITS[s]))

    chain.add(kv_sums)
    states(0)
    inside(0)
    chain.add(sums[0])
    add_only(chain)
    states(1)
    inside(1)
    settle(kv_sums)
    last(0)
    chain.add(sums[1])
    add_only(chain)
    last(1)
    outs = None
    for s, (f, n) in enumerate(zip(firsts, SPLITS)):
        outs = finish(
            chain, key_rows, value_rows, (own_grad, near_grad, *crossing[s]),
            (own_part, near_part, far_part[s]), (near_state, far_state[s]),
            local, kv_sums.parts, sums[s].parts, lasts[s], f, n, chunk, factor, outs,
        )
    return tuple(outs)


def solution(mesh):
    return jax.shard_map(
        functools.partial(body, mesh.shape["seq"], mesh.shape["head"]),
        mesh=mesh,
        in_specs=(P("seq", "head"), P("seq", "head"), P("seq", "head"), P(("seq", "head"), None)),
        out_specs=(P("seq", "head"), P("seq", "head"), P("seq", "head")),
        check_vma=False,
    )
```

```python
import functools
import math

import jax
import jax.numpy as jnp
from jax import lax
from jax.experimental import pallas as pl
from jax.experimental.pallas import tpu as pltpu
from jax.sharding import PartitionSpec as P

HEAD_DIM = 128
SPLITS = (4, 2, 2)
ORDER = "S0 I0 K A0 S1 I1 S2 A1 L0 I2 A2 L1 L2 F0 F1 F2"
COST = (10**10, 10**8)
F32 = jnp.float32
BF16 = jnp.bfloat16
NN = (((1,), (0,)), ((), ()))
NT = (((1,), (1,)), ((), ()))
TN = (((0,), (0,)), ((), ()))
VMEM = pl.BlockSpec(memory_space=pltpu.VMEM)
ANY = pl.BlockSpec(memory_space=pl.ANY)


def dot(a, b, dims):
    return lax.dot_general(a, b, dims, preferred_element_type=F32)


def head_cols(h):
    return slice(h * HEAD_DIM, (h + 1) * HEAD_DIM)


def rows_of(here, piece, chunk):
    return pl.ds(pl.multiple_of(here[0][piece] * chunk, chunk), chunk)


def place_as(array, spec):
    return pltpu.with_memory_space_constraint(array, pltpu.VMEM if spec is VMEM else pltpu.HBM)


class Chain:
    def __init__(self, token, head_size, seq_size):
        self.token = token
        self.head_size, self.seq_bits = head_size, seq_size.bit_length() - 1
        self.waits = []
        self.jobs = []
        self.through = []

    def add(self, *sums):
        self.jobs += [one for one in sums if not one.closed]

    def wait(self, *arrays):
        self.waits += arrays

    def __call__(self, name, kernel, operands, in_specs, out_shape, out_specs, grid=(), scratch=(), alias=None, cost=COST):
        extra = [self.token, *self.waits]
        jobs, self.waits, self.jobs = self.jobs, [], []
        skip, count = len(extra), len(operands)
        through, self.through = self.through, []
        pairs = [array for sums in jobs for array in (sums.window, sums.parts[-1])]
        operands, in_specs = [*operands, *pairs], [*in_specs, *[VMEM] * len(pairs)]
        out_shape = [*[bf16(*sums.window.shape) for sums in jobs], *out_shape]
        out_specs = [*[VMEM] * len(jobs), *out_specs, *[VMEM] * len(through)]
        out_shape += [bf16(*array.shape) for array in through]
        operands, in_specs = [*operands, *through], [*in_specs, *[VMEM] * len(through)]

        def run(*refs):
            rank, seq = lax.axis_index("head"), lax.axis_index("seq")
            place = [rank ^ mask for mask in range(self.head_size)]
            bits = [lax.shift_right_logical(seq, r) & 1 for r in range(self.seq_bits)]
            ins = refs[skip : skip + count]
            pair_refs = refs[skip + count : skip + count + len(pairs)]
            outs = refs[skip + len(operands) + 1 :]
            for n in range(len(jobs)):
                outs[n][...] = pair_refs[2 * n][...] + pair_refs[2 * n + 1][...]
            kernel((place, bits), *ins, *outs[len(jobs) : len(outs) - len(through)])

        aliases = {0: 0}
        for n in range(len(through)):
            aliases[skip + len(operands) - 1 - n] = len(out_shape) - n
        for source, target in (alias or {}).items():
            aliases[skip + source] = 1 + len(jobs) + target
        self.token, *outs = pl.pallas_call(
            run,
            grid=grid,
            in_specs=[ANY] * skip + list(in_specs),
            out_specs=[ANY] + list(out_specs),
            scratch_shapes=list(scratch),
            out_shape=[jax.ShapeDtypeStruct((8, 128), F32)] + list(out_shape),
            input_output_aliases=aliases,
            compiler_params=pltpu.CompilerParams(vmem_limit_bytes=8 * 1024 * 1024),
            cost_estimate=pl.CostEstimate(flops=cost[0], bytes_accessed=cost[1], transcendentals=0),
            name=name,
        )(*extra, *[place_as(x, s) for x, s in zip(operands, in_specs)])
        for sums, window in zip(jobs, outs):
            sums.window = window
            if sums.more():
                sums.go()
            else:
                sums.closed = True
        self.passed = outs[len(outs) - len(through) :]
        return outs[len(jobs) : len(outs) - len(through)]


def bf16(*shape):
    return pltpu.VMEM(shape, BF16)


def cut(chain, out_grads, parts):
    chunk = out_grads.shape[0]
    width = out_grads.shape[1] // chain.head_size

    def kernel(here, g_ref, *refs):
        outs, sems = refs[:-1], refs[-1]
        copies = []
        for n, (mask, head0, heads) in enumerate(parts):
            start = here[0][mask] * width + head0 * HEAD_DIM
            cols = pl.ds(pl.multiple_of(start, HEAD_DIM), heads * HEAD_DIM)
            copies.append(pltpu.make_async_copy(g_ref.at[:, cols], outs[n], sems.at[n]))
        for copy in copies:
            copy.start()
        for copy in copies:
            copy.wait()

    return chain(
        "cut", kernel, [out_grads], [ANY],
        [bf16(chunk, heads * HEAD_DIM) for _, _, heads in parts], [VMEM] * len(parts),
        scratch=[pltpu.SemaphoreType.DMA((len(parts),))],
    )


def kv_states(chain, key_rows, value_rows, chunk):
    rows, width = key_rows.shape
    heads, chunks = width // HEAD_DIM, rows // chunk

    def kernel(here, k_ref, v_ref, local_ref, total_ref):
        for h in range(heads):
            run = jnp.zeros((HEAD_DIM, HEAD_DIM), F32)
            for c in range(chunks):
                at = slice(c * chunk, (c + 1) * chunk)
                local_ref[c, h] = run.astype(BF16)
                run = run + dot(v_ref[at, head_cols(h)], k_ref[at, head_cols(h)], TN)
            total_ref[h] = run.astype(BF16)

    return chain(
        "kv_states", kernel, [key_rows, value_rows], [VMEM] * 2,
        [bf16(chunks, heads, HEAD_DIM, HEAD_DIM), bf16(heads, HEAD_DIM, HEAD_DIM)], [VMEM] * 2,
    )


def intra(chain, pieces, arrays, grads, head0, heads, chunk):
    count = len(pieces)

    def kernel(here, q_ref, k_ref, v_ref, *refs):
        g_refs, outs = refs[:count], refs[count:]
        row = lax.broadcasted_iota(jnp.int32, (chunk, chunk), 0)
        col = lax.broadcasted_iota(jnp.int32, (chunk, chunk), 1)
        upper, lower = row <= col, row >= col
        for n, piece in enumerate(pieces):
            rows = rows_of(here, piece, chunk)
            for h in range(heads):
                cols, own = head_cols(head0 + h), head_cols(h)
                q, k, v, g = q_ref[rows, cols], k_ref[rows, cols], v_ref[rows, cols], g_refs[n][:, own]
                fwd = jnp.where(upper, dot(k, q, NT), 0.0).astype(BF16)
                back = jnp.where(upper, dot(v, g, NT), 0.0).astype(BF16)
                turned = jnp.where(lower, dot(g, v, NT), 0.0).astype(BF16)
                outs[0][n, :, own] = dot(turned, k, NN).astype(BF16)
                outs[1][n, :, own] = dot(back, q, NN).astype(BF16)
                outs[2][n, :, own] = dot(fwd, g, NN).astype(BF16)

    shapes = [bf16(count, chunk, heads * HEAD_DIM)] * 3
    return chain(
        "intra", kernel, [*arrays, *grads], [VMEM] * (3 + count), shapes, [VMEM] * len(shapes)
    )


def near_states(chain, query_rows, grads, chunk):
    heads = query_rows.shape[1] // HEAD_DIM

    def kernel(here, q_ref, g0, g1, state_ref):
        for h in range(heads):
            cols = head_cols(h)
            for n, g_ref in enumerate((g0, g1)):
                q = q_ref[rows_of(here, n, chunk), cols]
                state_ref[n, h] = dot(q, g_ref[:, cols], TN).astype(BF16)

    return chain(
        "near_states", kernel, [query_rows, *grads], [VMEM] * 3,
        [bf16(2, heads, HEAD_DIM, HEAD_DIM)], [VMEM],
    )[0]


def far_states(chain, query_rows, grads, near, head0, heads, chunk):
    def kernel(here, q_ref, g0, g1, near_ref, state_ref, total_ref):
        for h in range(heads):
            cols, own = head_cols(head0 + h), head_cols(h)
            a = dot(q_ref[rows_of(here, 2, chunk), cols], g0[:, own], TN)
            b = dot(q_ref[rows_of(here, 3, chunk), cols], g1[:, own], TN)
            state_ref[0, h] = a.astype(BF16)
            state_ref[1, h] = b.astype(BF16)
            total = a + b + near_ref[0, head0 + h].astype(F32) + near_ref[1, head0 + h].astype(F32)
            total_ref[h] = total.astype(BF16)

    return chain(
        "far_states", kernel, [query_rows, *grads, near], [VMEM] * 4,
        [bf16(2, heads, HEAD_DIM, HEAD_DIM), bf16(heads, HEAD_DIM, HEAD_DIM)], [VMEM] * 2,
    )


def finish(chain, key_rows, value_rows, grads, parts, states, local, kv_in, grad_in, last, head0, heads, chunk, factor, outs):
    rows, feat = key_rows.shape
    rounds = len(kv_in)

    def kernel(here, *refs):
        refs = list(refs)
        if outs is not None:
            refs = refs[3:]

        def take(n):
            got = refs[:n]
            del refs[:n]
            return got

        k_ref, v_ref = take(2)
        g_refs = take(4)
        part_refs = [take(3), take(3), take(3)]
        state_refs = take(2)
        (local_ref,) = take(1)
        kv_refs, grad_refs = take(rounds), take(rounds)
        (last_ref,) = take(1)
        dq_ref, dk_ref, dv_ref = refs
        h = pl.program_id(0)
        bit = here[1][rounds].astype(F32)
        got = last_ref[h].astype(F32)
        prefix, suffix = got * bit, got * (1.0 - bit)
        for r in range(rounds):
            bit = here[1][r].astype(F32)
            prefix = prefix + kv_refs[r][head0 + h].astype(F32) * bit
            suffix = suffix + grad_refs[r][h].astype(F32) * (1.0 - bit)
        wide = pl.ds(pl.multiple_of((head0 + h) * HEAD_DIM, HEAD_DIM), HEAD_DIM)
        narrow = pl.ds(pl.multiple_of(h * HEAD_DIM, HEAD_DIM), HEAD_DIM)
        state = [
            state_refs[0][0, head0 + h], state_refs[0][1, head0 + h],
            state_refs[1][0, h], state_refs[1][1, h],
        ]
        state = [s.astype(F32) for s in state]
        for piece in range(4):
            place = here[0][piece]
            at = rows_of(here, piece, chunk)
            part, slot = part_refs[min(piece, 2)], max(piece - 2, 0)
            cols = wide if piece < 2 else narrow
            before_low = (prefix + local_ref[place, head0 + h].astype(F32)).astype(BF16)
            after = suffix
            for other in range(4):
                if other != piece:
                    later = (here[0][other] > place).astype(F32)
                    after = after + later * state[other]
            after_low = after.astype(BF16)
            out = part[0][slot, :, cols].astype(F32) + dot(g_refs[piece][:, cols], before_low, NN)
            dq_ref[at, :] = (factor * out).astype(BF16)
            out = part[1][slot, :, cols].astype(F32) + dot(v_ref[at, wide], after_low, NT)
            dk_ref[at, :] = (factor * out).astype(BF16)
            out = part[2][slot, :, cols].astype(F32) + dot(k_ref[at, wide], after_low, NN)
            dv_ref[at, :] = (factor * out).astype(BF16)

    operands = [key_rows, value_rows, *grads]
    for p in parts:
        operands += p
    operands += [*states, local, *kv_in, *grad_in, last]
    in_specs = [VMEM] * len(operands)
    alias = {}
    if outs is not None:
        operands = [*outs, *operands]
        in_specs = [ANY] * 3 + in_specs
        alias = {0: 0, 1: 1, 2: 2}
    return chain(
        "finish", kernel, operands, in_specs, [pltpu.HBM((rows, feat), BF16)] * 3,
        [pl.BlockSpec((rows, HEAD_DIM), lambda i: (0, i + head0))] * 3,
        grid=(heads,), alias=alias,
    )


class SeqSums:
    def __init__(self, total, axis, size):
        self.window, self.axis, self.size = total, axis, size
        self.step, self.parts, self.closed = 1, [], False

    def swap(self, block):
        got = lax.ppermute(block, self.axis, [(i, i ^ self.step) for i in range(self.size)])
        self.step *= 2
        return got

    def more(self):
        return 2 * self.step < self.size

    def go(self):
        self.parts.append(self.swap(self.window))


def add_only(chain):
    if chain.jobs:
        chain("add", lambda here: None, [], [], [], [])


def last_round(chain, prefix_sums, suffix_sums, head0, heads):
    rounds = len(suffix_sums.parts)

    def kernel(here, kv_ref, grad_a, grad_b, out_ref):
        upper = here[1][rounds] == 1

        @pl.when(upper)
        def _():
            out_ref[...] = grad_a[...] + grad_b[...]

        @pl.when(jnp.logical_not(upper))
        def _():
            out_ref[...] = kv_ref[head0 : head0 + heads]

    operands = [prefix_sums.window, suffix_sums.window, suffix_sums.parts[-1]]
    block = chain("last_round", kernel, operands, [VMEM] * 3, [bf16(heads, HEAD_DIM, HEAD_DIM)], [VMEM])[0]
    return suffix_sums.swap(block)


def body(seq_size, head_size, query_rows, key_rows, value_rows, out_grads):
    rows, feat = query_rows.shape
    chunk = rows // head_size
    head_count = feat // HEAD_DIM
    factor = 1.0 / math.sqrt(HEAD_DIM * rows * seq_size)
    chain = Chain(jnp.zeros((8, 128), F32), head_size, seq_size)
    arrays = (query_rows, key_rows, value_rows)
    firsts = [sum(SPLITS[:s]) for s in range(len(SPLITS))]

    def send(block, mask):
        return lax.ppermute(block, "head", [(i, i ^ mask) for i in range(head_size)])

    f, n = firsts[0], SPLITS[0]
    near_block, *blocks = cut(chain, out_grads, [(1, 0, head_count), (2, f, n), (3, f, n)])
    near_grad = send(near_block, 1)
    crossing = [[send(blocks[0], 2), send(blocks[1], 3)]]
    local, kv_total = kv_states(chain, key_rows, value_rows, chunk)
    kv_sums = SeqSums(kv_total, "seq", seq_size)
    kv_sums.go()
    chain.wait(near_grad)
    wanted = [(0, 0, head_count)]
    for f, n in zip(firsts[1:], SPLITS[1:]):
        wanted += [(2, f, n), (3, f, n)]
    own_grad, *blocks = cut(chain, out_grads, wanted)
    crossing.append([send(blocks[0], 2), send(blocks[1], 3)])
    later = blocks[2:]
    own_part = intra(chain, [0], arrays, [own_grad], 0, head_count, chunk)
    chain.add(kv_sums)
    near_state = near_states(chain, query_rows, (own_grad, near_grad), chunk)
    near_part = intra(chain, [1], arrays, [near_grad], 0, head_count, chunk)

    far_state, far_part, sums, lasts, outs = [], [], [], [], None

    def states(s):
        f, n = firsts[s], SPLITS[s]
        if s + 2 < len(SPLITS):
            chain.through = later[2 * s : 2 * s + 2]
        far, total = far_states(chain, query_rows, crossing[s], near_state, f, n, chunk)
        far_state.append(far)
        if s + 2 < len(SPLITS):
            crossing.append([send(chain.passed[0], 2), send(chain.passed[1], 3)])
        sums.append(SeqSums(total, "seq", seq_size))
        sums[s].go()

    def settle(one):
        while one.more():
            chain.add(one)
            add_only(chain)

    for step in ORDER.split():
        s = int(step[1:] or 0)
        if step[0] == "K":
            chain.add(kv_sums)
        elif step[0] == "S":
            states(s)
        elif step[0] == "I":
            far_part.append(intra(chain, [2, 3], arrays, crossing[s], firsts[s], SPLITS[s], chunk))
        elif step[0] == "A":
            chain.add(sums[s])
            add_only(chain)
        elif step[0] == "L":
            settle(sums[s])
            while not kv_sums.closed:
                chain.add(kv_sums)
                add_only(chain)
            lasts.append(last_round(chain, kv_sums, sums[s], firsts[s], SPLITS[s]))
        else:
            outs = finish(
                chain, key_rows, value_rows, (own_grad, near_grad, *crossing[s]),
                (own_part, near_part, far_part[s]), (near_state, far_state[s]),
                local, kv_sums.parts, sums[s].parts, lasts[s], firsts[s], SPLITS[s], chunk, factor, outs,
            )
    return tuple(outs)


def solution(mesh):
    return jax.shard_map(
        functools.partial(body, mesh.shape["seq"], mesh.shape["head"]),
        mesh=mesh,
        in_specs=(P("seq", "head"), P("seq", "head"), P("seq", "head"), P(("seq", "head"), None)),
        out_specs=(P("seq", "head"), P("seq", "head"), P("seq", "head")),
        check_vma=False,
    )
```

```python
import functools
import math

import jax
import jax.numpy as jnp
from jax import lax
from jax.experimental import pallas as pl
from jax.experimental.pallas import tpu as pltpu
from jax.sharding import PartitionSpec as P

HEAD_DIM = 128
SPLITS = (4, 2, 2)
ORDER = (
    ("S", 0), ("N", 0), ("K", 0), ("A", 0), ("S", 1), ("I", 0),
    ("S", 2), ("A", 1), ("L", 0), ("I", 1), ("A", 2), ("I", 2),
    ("L", 1), ("L", 2), ("F", 0), ("F", 1), ("F", 2),
)
COST = (10**10, 10**8)
F32 = jnp.float32
BF16 = jnp.bfloat16
NN = (((1,), (0,)), ((), ()))
NT = (((1,), (1,)), ((), ()))
TN = (((0,), (0,)), ((), ()))
VMEM = pl.BlockSpec(memory_space=pltpu.VMEM)
ANY = pl.BlockSpec(memory_space=pl.ANY)


def dot(a, b, dims):
    return lax.dot_general(a, b, dims, preferred_element_type=F32)


def head_cols(h):
    return slice(h * HEAD_DIM, (h + 1) * HEAD_DIM)


def rows_of(here, piece, chunk):
    return pl.ds(pl.multiple_of(here[0][piece] * chunk, chunk), chunk)


def place_as(array, spec):
    return pltpu.with_memory_space_constraint(array, pltpu.VMEM if spec is VMEM else pltpu.HBM)


class Chain:
    def __init__(self, token, head_size, seq_size, factor):
        self.token, self.factor = token, factor
        self.head_size, self.seq_bits = head_size, seq_size.bit_length() - 1
        self.waits = []
        self.jobs = []
        self.through = []

    def add(self, *sums):
        self.jobs += [one for one in sums if not one.closed]

    def wait(self, *arrays):
        self.waits += arrays

    def __call__(self, name, kernel, operands, in_specs, out_shape, out_specs, grid=(), scratch=(), alias=None, cost=COST):
        extra = [self.token, *self.waits]
        jobs, self.waits, self.jobs = self.jobs, [], []
        skip, count = len(extra), len(operands)
        through, self.through = self.through, []
        results = len(jobs) + len(out_shape)
        pairs = [array for sums in jobs for array in (sums.window, sums.parts[-1])]
        operands, in_specs = [*operands, *pairs], [*in_specs, *[VMEM] * len(pairs)]
        out_shape = [*[bf16(*sums.window.shape) for sums in jobs], *out_shape]
        out_specs = [*[VMEM] * len(jobs), *out_specs, *[VMEM] * len(through)]
        out_shape += [bf16(*array.shape) for array in through]
        operands, in_specs = [*operands, *through], [*in_specs, *[VMEM] * len(through)]

        def run(*refs):
            rank, seq = lax.axis_index("head"), lax.axis_index("seq")
            place = [rank ^ mask for mask in range(self.head_size)]
            bits = [lax.shift_right_logical(seq, r) & 1 for r in range(self.seq_bits)]
            ins = refs[skip : skip + count]
            pair_refs = refs[skip + count : skip + count + len(pairs)]
            outs = refs[skip + len(operands) + 1 :]
            for n in range(len(jobs)):
                outs[n][...] = pair_refs[2 * n][...] + pair_refs[2 * n + 1][...]
            kernel((place, bits), *ins, *outs[len(jobs) : results], *outs[results + len(through) :])

        aliases = {0: 0}
        for n in range(len(through)):
            aliases[skip + len(operands) - 1 - n] = len(out_shape) - n
        for source, target in (alias or {}).items():
            aliases[skip + source] = 1 + len(jobs) + target
        self.token, *outs = pl.pallas_call(
            run,
            grid=grid,
            in_specs=[ANY] * skip + list(in_specs),
            out_specs=[ANY] + list(out_specs),
            scratch_shapes=list(scratch),
            out_shape=[jax.ShapeDtypeStruct((8, 128), F32)] + list(out_shape),
            input_output_aliases=aliases,
            compiler_params=pltpu.CompilerParams(vmem_limit_bytes=8 * 1024 * 1024),
            cost_estimate=pl.CostEstimate(flops=cost[0], bytes_accessed=cost[1], transcendentals=0),
            name=name,
        )(*extra, *[place_as(x, s) for x, s in zip(operands, in_specs)])
        for sums, window in zip(jobs, outs):
            sums.window = window
            if sums.more():
                sums.go()
            else:
                sums.closed = True
        self.passed = outs[len(outs) - len(through) :]
        return outs[len(jobs) : len(outs) - len(through)]


def bf16(*shape):
    return pltpu.VMEM(shape, BF16)


def cut(chain, out_grads, parts):
    chunk = out_grads.shape[0]
    width = out_grads.shape[1] // chain.head_size

    def kernel(here, g_ref, *refs):
        outs, sems = refs[:-1], refs[-1]
        copies = []
        for n, (mask, head0, heads) in enumerate(parts):
            start = here[0][mask] * width + head0 * HEAD_DIM
            cols = pl.ds(pl.multiple_of(start, HEAD_DIM), heads * HEAD_DIM)
            copies.append(pltpu.make_async_copy(g_ref.at[:, cols], outs[n], sems.at[n]))
        for copy in copies:
            copy.start()
        for copy in copies:
            copy.wait()

    return chain(
        "cut", kernel, [out_grads], [ANY],
        [bf16(chunk, heads * HEAD_DIM) for _, _, heads in parts], [VMEM] * len(parts),
        scratch=[pltpu.SemaphoreType.DMA((len(parts),))],
    )


def kv_states(chain, key_rows, value_rows, chunk):
    rows, width = key_rows.shape
    heads, chunks = width // HEAD_DIM, rows // chunk

    def kernel(here, k_ref, v_ref, local_ref, total_ref):
        for h in range(heads):
            run = jnp.zeros((HEAD_DIM, HEAD_DIM), F32)
            for c in range(chunks):
                at = slice(c * chunk, (c + 1) * chunk)
                local_ref[c, h] = run.astype(BF16)
                run = run + chain.factor * dot(v_ref[at, head_cols(h)], k_ref[at, head_cols(h)], TN)
            total_ref[h] = run.astype(BF16)

    return chain(
        "kv_states", kernel, [key_rows, value_rows], [VMEM] * 2,
        [bf16(chunks, heads, HEAD_DIM, HEAD_DIM), bf16(heads, HEAD_DIM, HEAD_DIM)], [VMEM] * 2,
    )


def intra(chain, pieces, arrays, grads, head0, heads, chunk):
    count = len(pieces)

    def kernel(here, q_ref, k_ref, v_ref, *refs):
        g_refs, outs = refs[:count], refs[count:]
        row = lax.broadcasted_iota(jnp.int32, (chunk, chunk), 0)
        col = lax.broadcasted_iota(jnp.int32, (chunk, chunk), 1)
        upper = jnp.where(row <= col, chain.factor, 0.0)
        lower = jnp.where(row >= col, chain.factor, 0.0)
        for n, piece in enumerate(pieces):
            rows = rows_of(here, piece, chunk)
            for h in range(heads):
                cols, own = head_cols(head0 + h), head_cols(h)
                q, k, v, g = q_ref[rows, cols], k_ref[rows, cols], v_ref[rows, cols], g_refs[n][:, own]
                fwd = (upper * dot(k, q, NT)).astype(BF16)
                back = (upper * dot(v, g, NT)).astype(BF16)
                turned = (lower * dot(g, v, NT)).astype(BF16)
                outs[0][n, :, own] = dot(turned, k, NN).astype(BF16)
                outs[1][n, :, own] = dot(back, q, NN).astype(BF16)
                outs[2][n, :, own] = dot(fwd, g, NN).astype(BF16)

    shapes = [bf16(count, chunk, heads * HEAD_DIM)] * 3
    return chain(
        "intra", kernel, [*arrays, *grads], [VMEM] * (3 + count), shapes, [VMEM] * len(shapes)
    )


def near_states(chain, query_rows, grads, chunk):
    heads = query_rows.shape[1] // HEAD_DIM

    def kernel(here, q_ref, g0, g1, state_ref):
        for h in range(heads):
            cols = head_cols(h)
            for n, g_ref in enumerate((g0, g1)):
                q = q_ref[rows_of(here, n, chunk), cols]
                state_ref[n, h] = (chain.factor * dot(q, g_ref[:, cols], TN)).astype(BF16)

    return chain(
        "near_states", kernel, [query_rows, *grads], [VMEM] * 3,
        [bf16(2, heads, HEAD_DIM, HEAD_DIM)], [VMEM],
    )[0]


def far_states(chain, query_rows, grads, near, head0, heads, chunk):
    def kernel(here, q_ref, g0, g1, near_ref, state_ref, total_ref):
        for h in range(heads):
            cols, own = head_cols(head0 + h), head_cols(h)
            a = chain.factor * dot(q_ref[rows_of(here, 2, chunk), cols], g0[:, own], TN)
            b = chain.factor * dot(q_ref[rows_of(here, 3, chunk), cols], g1[:, own], TN)
            state_ref[0, h] = a.astype(BF16)
            state_ref[1, h] = b.astype(BF16)
            total = a + b + near_ref[0, head0 + h].astype(F32) + near_ref[1, head0 + h].astype(F32)
            total_ref[h] = total.astype(BF16)

    return chain(
        "far_states", kernel, [query_rows, *grads, near], [VMEM] * 4,
        [bf16(2, heads, HEAD_DIM, HEAD_DIM), bf16(heads, HEAD_DIM, HEAD_DIM)], [VMEM] * 2,
    )


def finish(chain, key_rows, value_rows, grads, parts, states, local, kv_in, grad_in, last, head0, heads, chunk, outs):
    rows, feat = key_rows.shape
    rounds = len(kv_in)

    def kernel(here, *refs):
        refs = list(refs)
        if outs is not None:
            refs = refs[3:]

        def take(n):
            got = refs[:n]
            del refs[:n]
            return got

        k_ref, v_ref = take(2)
        g_refs = take(4)
        part_refs = [take(3), take(3), take(3)]
        state_refs = take(2)
        (local_ref,) = take(1)
        kv_refs, grad_refs = take(rounds), take(rounds)
        (last_ref,) = take(1)
        out_refs, refs = refs[:3], refs[3:]
        low_ref, stage_refs, sems = refs[0], refs[1:4], refs[4]
        for h in range(heads):
            bit = here[1][rounds].astype(F32)
            got = last_ref[h].astype(F32)
            prefix, suffix = got * bit, got * (1.0 - bit)
            for r in range(rounds):
                bit = here[1][r].astype(F32)
                prefix = prefix + kv_refs[r][head0 + h].astype(F32) * bit
                suffix = suffix + grad_refs[r][h].astype(F32) * (1.0 - bit)
            state = [
                state_refs[0][0, head0 + h], state_refs[0][1, head0 + h],
                state_refs[1][0, h], state_refs[1][1, h],
            ]
            state = [s.astype(F32) for s in state]
            halves = [state[0] + state[1], state[2] + state[3]]
            for piece in range(4):
                place = here[0][piece]
                half = piece // 2
                far = (here[0][2 - 2 * half] > here[0][2 * half]).astype(F32)
                near = (here[0][piece ^ 1] > place).astype(F32)
                low_ref[0, piece, h] = (prefix + local_ref[place, head0 + h].astype(F32)).astype(BF16)
                low_ref[1, piece, h] = (suffix + far * halves[1 - half] + near * state[piece ^ 1]).astype(BF16)
        copies = []
        target = slice(head0 * HEAD_DIM, (head0 + heads) * HEAD_DIM)
        for piece in range(4):
            at = rows_of(here, piece, chunk)
            part, slot = part_refs[min(piece, 2)], max(piece - 2, 0)
            for h in range(heads):
                wide, narrow = head_cols(head0 + h), head_cols(h)
                cols = wide if piece < 2 else narrow
                before_low, after_low = low_ref[0, piece, h], low_ref[1, piece, h]
                out = part[0][slot, :, cols].astype(F32) + dot(g_refs[piece][:, cols], before_low, NN)
                stage_refs[0][piece, :, narrow] = out.astype(BF16)
                out = part[1][slot, :, cols].astype(F32) + dot(v_ref[at, wide], after_low, NT)
                stage_refs[1][piece, :, narrow] = out.astype(BF16)
                out = part[2][slot, :, cols].astype(F32) + dot(k_ref[at, wide], after_low, NN)
                stage_refs[2][piece, :, narrow] = out.astype(BF16)
            for n in range(3):
                copy = pltpu.make_async_copy(
                    stage_refs[n].at[piece], out_refs[n].at[at, target], sems.at[n, piece]
                )
                copy.start()
                copies.append(copy)
        for copy in copies:
            copy.wait()

    operands = [key_rows, value_rows, *grads]
    for p in parts:
        operands += p
    operands += [*states, local, *kv_in, *grad_in, last]
    in_specs = [VMEM] * len(operands)
    alias = {}
    if outs is not None:
        operands = [*outs, *operands]
        in_specs = [ANY] * 3 + in_specs
        alias = {0: 0, 1: 1, 2: 2}
    return chain(
        "finish", kernel, operands, in_specs, [pltpu.HBM((rows, feat), BF16)] * 3,
        [ANY] * 3, alias=alias,
        scratch=[
            pltpu.VMEM((2, 4, heads, HEAD_DIM, HEAD_DIM), BF16),
            *[pltpu.VMEM((4, chunk, heads * HEAD_DIM), BF16)] * 3,
            pltpu.SemaphoreType.DMA((3, 4)),
        ],
    )


class SeqSums:
    def __init__(self, total, axis, size):
        self.window, self.axis, self.size = total, axis, size
        self.step, self.parts, self.closed = 1, [], False

    def swap(self, block):
        got = lax.ppermute(block, self.axis, [(i, i ^ self.step) for i in range(self.size)])
        self.step *= 2
        return got

    def more(self):
        return 2 * self.step < self.size

    def go(self):
        self.parts.append(self.swap(self.window))


def add_only(chain):
    if chain.jobs:
        chain("add", lambda here: None, [], [], [], [])


def last_round(chain, prefix_sums, suffix_sums, head0, heads):
    rounds = len(suffix_sums.parts)

    def kernel(here, kv_ref, grad_a, grad_b, out_ref):
        upper = here[1][rounds] == 1

        @pl.when(upper)
        def _():
            out_ref[...] = grad_a[...] + grad_b[...]

        @pl.when(jnp.logical_not(upper))
        def _():
            out_ref[...] = kv_ref[head0 : head0 + heads]

    operands = [prefix_sums.window, suffix_sums.window, suffix_sums.parts[-1]]
    block = chain("last_round", kernel, operands, [VMEM] * 3, [bf16(heads, HEAD_DIM, HEAD_DIM)], [VMEM])[0]
    return suffix_sums.swap(block)


def body(seq_size, head_size, query_rows, key_rows, value_rows, out_grads):
    rows, feat = query_rows.shape
    chunk = rows // head_size
    head_count = feat // HEAD_DIM
    factor = 1.0 / math.sqrt(HEAD_DIM * rows * seq_size)
    chain = Chain(jnp.zeros((8, 128), F32), head_size, seq_size, factor)
    arrays = (query_rows, key_rows, value_rows)
    firsts = [sum(SPLITS[:s]) for s in range(len(SPLITS))]

    def send(block, mask):
        return lax.ppermute(block, "head", [(i, i ^ mask) for i in range(head_size)])

    f, n = firsts[0], SPLITS[0]
    near_block, *blocks = cut(chain, out_grads, [(1, 0, head_count), (2, f, n), (3, f, n)])
    near_grad = send(near_block, 1)
    crossing = [[send(blocks[0], 2), send(blocks[1], 3)]]
    local, kv_total = kv_states(chain, key_rows, value_rows, chunk)
    kv_sums = SeqSums(kv_total, "seq", seq_size)
    kv_sums.go()
    chain.wait(near_grad)
    wanted = [(0, 0, head_count)]
    for f, n in zip(firsts[1:], SPLITS[1:]):
        wanted += [(2, f, n), (3, f, n)]
    own_grad, *blocks = cut(chain, out_grads, wanted)
    crossing.append([send(blocks[0], 2), send(blocks[1], 3)])
    later = blocks[2:]
    own_part = intra(chain, [0], arrays, [own_grad], 0, head_count, chunk)
    chain.add(kv_sums)
    near_state = near_states(chain, query_rows, (own_grad, near_grad), chunk)
    far_state, far_part, sums, lasts, outs = [], [], [], [], None

    def states(s):
        f, n = firsts[s], SPLITS[s]
        far, total = far_states(chain, query_rows, crossing[s], near_state, f, n, chunk)
        far_state.append(far)
        sums.append(SeqSums(total, "seq", seq_size))
        sums[s].go()

    def settle(one):
        while one.more():
            chain.add(one)
            add_only(chain)

    for step, s in ORDER:
        if step == "K":
            chain.add(kv_sums)
        elif step == "N":
            chain.through = later
            near_part = intra(chain, [1], arrays, [near_grad], 0, head_count, chunk)
            for n in range(0, len(later), 2):
                crossing.append([send(chain.passed[n], 2), send(chain.passed[n + 1], 3)])
        elif step == "S":
            states(s)
        elif step == "I":
            far_part.append(intra(chain, [2, 3], arrays, crossing[s], firsts[s], SPLITS[s], chunk))
        elif step == "A":
            chain.add(sums[s])
            add_only(chain)
        elif step == "L":
            settle(sums[s])
            while not kv_sums.closed:
                chain.add(kv_sums)
                add_only(chain)
            lasts.append(last_round(chain, kv_sums, sums[s], firsts[s], SPLITS[s]))
        else:
            outs = finish(
                chain, key_rows, value_rows, (own_grad, near_grad, *crossing[s]),
                (own_part, near_part, far_part[s]), (near_state, far_state[s]),
                local, kv_sums.parts, sums[s].parts, lasts[s], firsts[s], SPLITS[s], chunk, outs,
            )
    return tuple(outs)


def solution(mesh):
    return jax.shard_map(
        functools.partial(body, mesh.shape["seq"], mesh.shape["head"]),
        mesh=mesh,
        in_specs=(P("seq", "head"), P("seq", "head"), P("seq", "head"), P(("seq", "head"), None)),
        out_specs=(P("seq", "head"), P("seq", "head"), P("seq", "head")),
        check_vma=False,
    )
```

```python
import functools
import math

import jax
import jax.numpy as jnp
from jax import lax
from jax.experimental import pallas as pl
from jax.experimental.pallas import tpu as pltpu
from jax.sharding import PartitionSpec as P

HEAD_DIM = 128
SPLITS = (4, 2, 2)
ORDER = (
    ("S", 0), ("N", 0), ("K", 0), ("A", 0), ("S", 1), ("I", 0),
    ("S", 2), ("A", 1), ("L", 0), ("I", 1), ("A", 2), ("I", 2),
    ("L", 1), ("L", 2), ("F", 0), ("F", 1), ("F", 2),
)
COST = (14 * 10**9, 10**3)
F32 = jnp.float32
BF16 = jnp.bfloat16
NN = (((1,), (0,)), ((), ()))
NT = (((1,), (1,)), ((), ()))
TN = (((0,), (0,)), ((), ()))
VMEM = pl.BlockSpec(memory_space=pltpu.VMEM)
ANY = pl.BlockSpec(memory_space=pl.ANY)


def dot(a, b, dims):
    return lax.dot_general(a, b, dims, preferred_element_type=F32)


def head_cols(h):
    return slice(h * HEAD_DIM, (h + 1) * HEAD_DIM)


def rows_of(here, piece, chunk):
    return pl.ds(pl.multiple_of(here[0][piece] * chunk, chunk), chunk)


def place_as(array, spec):
    return pltpu.with_memory_space_constraint(array, pltpu.VMEM if spec is VMEM else pltpu.HBM)


class Chain:
    def __init__(self, token, head_size, seq_size, factor):
        self.token, self.factor = token, factor
        self.head_size, self.seq_bits = head_size, seq_size.bit_length() - 1
        self.waits = []
        self.jobs = []
        self.through = []

    def add(self, *sums):
        self.jobs += [one for one in sums if not one.closed]

    def wait(self, *arrays):
        self.waits += arrays

    def __call__(self, name, kernel, operands, in_specs, out_shape, out_specs, grid=(), scratch=(), alias=None, cost=COST):
        extra = [self.token, *self.waits]
        jobs, self.waits, self.jobs = self.jobs, [], []
        skip, count = len(extra), len(operands)
        through, self.through = self.through, []
        results = len(jobs) + len(out_shape)
        pairs = [array for sums in jobs for array in (sums.window, sums.parts[-1])]
        operands, in_specs = [*operands, *pairs], [*in_specs, *[VMEM] * len(pairs)]
        out_shape = [*[bf16(*sums.window.shape) for sums in jobs], *out_shape]
        out_specs = [*[VMEM] * len(jobs), *out_specs, *[VMEM] * len(through)]
        out_shape += [bf16(*array.shape) for array in through]
        operands, in_specs = [*operands, *through], [*in_specs, *[VMEM] * len(through)]

        def run(*refs):
            rank, seq = lax.axis_index("head"), lax.axis_index("seq")
            place = [rank ^ mask for mask in range(self.head_size)]
            bits = [lax.shift_right_logical(seq, r) & 1 for r in range(self.seq_bits)]
            ins = refs[skip : skip + count]
            pair_refs = refs[skip + count : skip + count + len(pairs)]
            outs = refs[skip + len(operands) + 1 :]
            for n in range(len(jobs)):
                outs[n][...] = pair_refs[2 * n][...] + pair_refs[2 * n + 1][...]
            kernel((place, bits), *ins, *outs[len(jobs) : results], *outs[results + len(through) :])

        aliases = {0: 0}
        for n in range(len(through)):
            aliases[skip + len(operands) - 1 - n] = len(out_shape) - n
        for source, target in (alias or {}).items():
            aliases[skip + source] = 1 + len(jobs) + target
        self.token, *outs = pl.pallas_call(
            run,
            grid=grid,
            in_specs=[ANY] * skip + list(in_specs),
            out_specs=[ANY] + list(out_specs),
            scratch_shapes=list(scratch),
            out_shape=[jax.ShapeDtypeStruct((8, 128), F32)] + list(out_shape),
            input_output_aliases=aliases,
            compiler_params=pltpu.CompilerParams(vmem_limit_bytes=8 * 1024 * 1024),
            cost_estimate=pl.CostEstimate(flops=cost[0], bytes_accessed=cost[1], transcendentals=0),
            name=name,
        )(*extra, *[place_as(x, s) for x, s in zip(operands, in_specs)])
        for sums, window in zip(jobs, outs):
            sums.window = window
            if sums.more():
                sums.go()
            else:
                sums.closed = True
        self.passed = outs[len(outs) - len(through) :]
        return outs[len(jobs) : len(outs) - len(through)]


def bf16(*shape):
    return pltpu.VMEM(shape, BF16)


def cut(chain, out_grads, parts):
    chunk = out_grads.shape[0]
    width = out_grads.shape[1] // chain.head_size

    def kernel(here, g_ref, *refs):
        outs, sems = refs[:-1], refs[-1]
        copies = []
        for n, (mask, head0, heads) in enumerate(parts):
            start = here[0][mask] * width + head0 * HEAD_DIM
            cols = pl.ds(pl.multiple_of(start, HEAD_DIM), heads * HEAD_DIM)
            copies.append(pltpu.make_async_copy(g_ref.at[:, cols], outs[n], sems.at[n]))
        for copy in copies:
            copy.start()
        for copy in copies:
            copy.wait()

    return chain(
        "cut", kernel, [out_grads], [ANY],
        [bf16(chunk, heads * HEAD_DIM) for _, _, heads in parts], [VMEM] * len(parts),
        scratch=[pltpu.SemaphoreType.DMA((len(parts),))],
    )


def kv_states(chain, key_rows, value_rows, chunk):
    rows, width = key_rows.shape
    heads, chunks = width // HEAD_DIM, rows // chunk

    def kernel(here, k_ref, v_ref, local_ref, total_ref):
        for h in range(heads):
            run = jnp.zeros((HEAD_DIM, HEAD_DIM), F32)
            for c in range(chunks):
                at = slice(c * chunk, (c + 1) * chunk)
                local_ref[c, h] = run.astype(BF16)
                run = run + chain.factor * dot(v_ref[at, head_cols(h)], k_ref[at, head_cols(h)], TN)
            total_ref[h] = run.astype(BF16)

    return chain(
        "kv_states", kernel, [key_rows, value_rows], [VMEM] * 2,
        [bf16(chunks, heads, HEAD_DIM, HEAD_DIM), bf16(heads, HEAD_DIM, HEAD_DIM)], [VMEM] * 2,
    )


def intra(chain, pieces, arrays, grads, head0, heads, chunk):
    count = len(pieces)

    def kernel(here, q_ref, k_ref, v_ref, *refs):
        g_refs, outs = refs[:count], refs[count:]
        row = lax.broadcasted_iota(jnp.int32, (chunk, chunk), 0)
        col = lax.broadcasted_iota(jnp.int32, (chunk, chunk), 1)
        upper = jnp.where(row <= col, chain.factor, 0.0)
        lower = jnp.where(row >= col, chain.factor, 0.0)
        for n, piece in enumerate(pieces):
            rows = rows_of(here, piece, chunk)
            for h in range(heads):
                cols, own = head_cols(head0 + h), head_cols(h)
                q, k, v, g = q_ref[rows, cols], k_ref[rows, cols], v_ref[rows, cols], g_refs[n][:, own]
                fwd = (upper * dot(k, q, NT)).astype(BF16)
                back = (upper * dot(v, g, NT)).astype(BF16)
                turned = (lower * dot(g, v, NT)).astype(BF16)
                outs[0][n, :, own] = dot(turned, k, NN).astype(BF16)
                outs[1][n, :, own] = dot(back, q, NN).astype(BF16)
                outs[2][n, :, own] = dot(fwd, g, NN).astype(BF16)

    shapes = [bf16(count, chunk, heads * HEAD_DIM)] * 3
    return chain(
        "intra", kernel, [*arrays, *grads], [VMEM] * (3 + count), shapes, [VMEM] * len(shapes)
    )


def near_states(chain, query_rows, grads, chunk):
    heads = query_rows.shape[1] // HEAD_DIM

    def kernel(here, q_ref, g0, g1, state_ref):
        for h in range(heads):
            cols = head_cols(h)
            for n, g_ref in enumerate((g0, g1)):
                q = q_ref[rows_of(here, n, chunk), cols]
                state_ref[n, h] = (chain.factor * dot(q, g_ref[:, cols], TN)).astype(BF16)

    return chain(
        "near_states", kernel, [query_rows, *grads], [VMEM] * 3,
        [bf16(2, heads, HEAD_DIM, HEAD_DIM)], [VMEM],
    )[0]


def far_states(chain, query_rows, grads, near, head0, heads, chunk):
    def kernel(here, q_ref, g0, g1, near_ref, state_ref, total_ref):
        for h in range(heads):
            cols, own = head_cols(head0 + h), head_cols(h)
            a = chain.factor * dot(q_ref[rows_of(here, 2, chunk), cols], g0[:, own], TN)
            b = chain.factor * dot(q_ref[rows_of(here, 3, chunk), cols], g1[:, own], TN)
            state_ref[0, h] = a.astype(BF16)
            state_ref[1, h] = b.astype(BF16)
            total = a + b + near_ref[0, head0 + h].astype(F32) + near_ref[1, head0 + h].astype(F32)
            total_ref[h] = total.astype(BF16)

    return chain(
        "far_states", kernel, [query_rows, *grads, near], [VMEM] * 4,
        [bf16(2, heads, HEAD_DIM, HEAD_DIM), bf16(heads, HEAD_DIM, HEAD_DIM)], [VMEM] * 2,
    )


def finish(chain, key_rows, value_rows, grads, parts, states, local, kv_in, grad_in, last, head0, heads, chunk, outs):
    rows, feat = key_rows.shape
    rounds = len(kv_in)

    def kernel(here, *refs):
        refs = list(refs)
        if outs is not None:
            refs = refs[3:]

        def take(n):
            got = refs[:n]
            del refs[:n]
            return got

        k_ref, v_ref = take(2)
        g_refs = take(4)
        part_refs = [take(3), take(3), take(3)]
        state_refs = take(2)
        (local_ref,) = take(1)
        kv_refs, grad_refs = take(rounds), take(rounds)
        (last_ref,) = take(1)
        out_refs, refs = refs[:3], refs[3:]
        low_ref, stage_refs, sems = refs[0], refs[1:4], refs[4]
        for h in range(heads):
            bit = here[1][rounds].astype(F32)
            got = last_ref[h].astype(F32)
            prefix, suffix = got * bit, got * (1.0 - bit)
            for r in range(rounds):
                bit = here[1][r].astype(F32)
                prefix = prefix + kv_refs[r][head0 + h].astype(F32) * bit
                suffix = suffix + grad_refs[r][h].astype(F32) * (1.0 - bit)
            state = [
                state_refs[0][0, head0 + h], state_refs[0][1, head0 + h],
                state_refs[1][0, h], state_refs[1][1, h],
            ]
            state = [s.astype(F32) for s in state]
            halves = [state[0] + state[1], state[2] + state[3]]
            for piece in range(4):
                place = here[0][piece]
                half = piece // 2
                far = (here[0][2 - 2 * half] > here[0][2 * half]).astype(F32)
                near = (here[0][piece ^ 1] > place).astype(F32)
                low_ref[0, piece, h] = (prefix + local_ref[place, head0 + h].astype(F32)).astype(BF16)
                low_ref[1, piece, h] = (suffix + far * halves[1 - half] + near * state[piece ^ 1]).astype(BF16)
        copies = []
        target = slice(head0 * HEAD_DIM, (head0 + heads) * HEAD_DIM)
        for piece in range(4):
            at = rows_of(here, piece, chunk)
            part, slot = part_refs[min(piece, 2)], max(piece - 2, 0)
            for h in range(heads):
                wide, narrow = head_cols(head0 + h), head_cols(h)
                cols = wide if piece < 2 else narrow
                before_low, after_low = low_ref[0, piece, h], low_ref[1, piece, h]
                out = part[0][slot, :, cols].astype(F32) + dot(g_refs[piece][:, cols], before_low, NN)
                stage_refs[0][piece, :, narrow] = out.astype(BF16)
                out = part[1][slot, :, cols].astype(F32) + dot(v_ref[at, wide], after_low, NT)
                stage_refs[1][piece, :, narrow] = out.astype(BF16)
                out = part[2][slot, :, cols].astype(F32) + dot(k_ref[at, wide], after_low, NN)
                stage_refs[2][piece, :, narrow] = out.astype(BF16)
            for n in range(3):
                copy = pltpu.make_async_copy(
                    stage_refs[n].at[piece], out_refs[n].at[at, target], sems.at[n, piece]
                )
                copy.start()
                copies.append(copy)
        for copy in copies:
            copy.wait()

    operands = [key_rows, value_rows, *grads]
    for p in parts:
        operands += p
    operands += [*states, local, *kv_in, *grad_in, last]
    in_specs = [VMEM] * len(operands)
    alias = {}
    if outs is not None:
        operands = [*outs, *operands]
        in_specs = [ANY] * 3 + in_specs
        alias = {0: 0, 1: 1, 2: 2}
    return chain(
        "finish", kernel, operands, in_specs, [pltpu.HBM((rows, feat), BF16)] * 3,
        [ANY] * 3, alias=alias,
        scratch=[
            pltpu.VMEM((2, 4, heads, HEAD_DIM, HEAD_DIM), BF16),
            *[pltpu.VMEM((4, chunk, heads * HEAD_DIM), BF16)] * 3,
            pltpu.SemaphoreType.DMA((3, 4)),
        ],
    )


class SeqSums:
    def __init__(self, total, axis, size):
        self.window, self.axis, self.size = total, axis, size
        self.step, self.parts, self.closed = 1, [], False

    def swap(self, block):
        got = lax.ppermute(block, self.axis, [(i, i ^ self.step) for i in range(self.size)])
        self.step *= 2
        return got

    def more(self):
        return 2 * self.step < self.size

    def go(self):
        self.parts.append(self.swap(self.window))


def add_only(chain):
    if chain.jobs:
        chain("add", lambda here: None, [], [], [], [])


def last_round(chain, prefix_sums, suffix_sums, head0, heads):
    rounds = len(suffix_sums.parts)

    def kernel(here, kv_ref, grad_a, grad_b, out_ref):
        upper = here[1][rounds] == 1

        @pl.when(upper)
        def _():
            out_ref[...] = grad_a[...] + grad_b[...]

        @pl.when(jnp.logical_not(upper))
        def _():
            out_ref[...] = kv_ref[head0 : head0 + heads]

    operands = [prefix_sums.window, suffix_sums.window, suffix_sums.parts[-1]]
    block = chain("last_round", kernel, operands, [VMEM] * 3, [bf16(heads, HEAD_DIM, HEAD_DIM)], [VMEM])[0]
    return suffix_sums.swap(block)


def body(seq_size, head_size, query_rows, key_rows, value_rows, out_grads):
    rows, feat = query_rows.shape
    chunk = rows // head_size
    head_count = feat // HEAD_DIM
    factor = 1.0 / math.sqrt(HEAD_DIM * rows * seq_size)
    chain = Chain(jnp.zeros((8, 128), F32), head_size, seq_size, factor)
    arrays = (query_rows, key_rows, value_rows)
    firsts = [sum(SPLITS[:s]) for s in range(len(SPLITS))]

    def send(block, mask):
        return lax.ppermute(block, "head", [(i, i ^ mask) for i in range(head_size)])

    f, n = firsts[0], SPLITS[0]
    near_block, *blocks = cut(chain, out_grads, [(1, 0, head_count), (2, f, n), (3, f, n)])
    near_grad = send(near_block, 1)
    crossing = [[send(blocks[0], 2), send(blocks[1], 3)]]
    local, kv_total = kv_states(chain, key_rows, value_rows, chunk)
    kv_sums = SeqSums(kv_total, "seq", seq_size)
    kv_sums.go()
    chain.wait(near_grad)
    wanted = [(0, 0, head_count)]
    for f, n in zip(firsts[1:], SPLITS[1:]):
        wanted += [(2, f, n), (3, f, n)]
    own_grad, *blocks = cut(chain, out_grads, wanted)
    crossing.append([send(blocks[0], 2), send(blocks[1], 3)])
    later = blocks[2:]
    own_part = intra(chain, [0], arrays, [own_grad], 0, head_count, chunk)
    chain.add(kv_sums)
    near_state = near_states(chain, query_rows, (own_grad, near_grad), chunk)
    far_state, far_part, sums, lasts, outs = [], [], [], [], None

    def states(s):
        f, n = firsts[s], SPLITS[s]
        far, total = far_states(chain, query_rows, crossing[s], near_state, f, n, chunk)
        far_state.append(far)
        sums.append(SeqSums(total, "seq", seq_size))
        sums[s].go()

    def settle(one):
        while one.more():
            chain.add(one)
            add_only(chain)

    for step, s in ORDER:
        if step == "K":
            chain.add(kv_sums)
        elif step == "N":
            chain.through = later
            near_part = intra(chain, [1], arrays, [near_grad], 0, head_count, chunk)
            for n in range(0, len(later), 2):
                crossing.append([send(chain.passed[n], 2), send(chain.passed[n + 1], 3)])
        elif step == "S":
            states(s)
        elif step == "I":
            far_part.append(intra(chain, [2, 3], arrays, crossing[s], firsts[s], SPLITS[s], chunk))
        elif step == "A":
            chain.add(sums[s])
            add_only(chain)
        elif step == "L":
            settle(sums[s])
            while not kv_sums.closed:
                chain.add(kv_sums)
                add_only(chain)
            lasts.append(last_round(chain, kv_sums, sums[s], firsts[s], SPLITS[s]))
        else:
            outs = finish(
                chain, key_rows, value_rows, (own_grad, near_grad, *crossing[s]),
                (own_part, near_part, far_part[s]), (near_state, far_state[s]),
                local, kv_sums.parts, sums[s].parts, lasts[s], firsts[s], SPLITS[s], chunk, outs,
            )
    return tuple(outs)


def solution(mesh):
    return jax.shard_map(
        functools.partial(body, mesh.shape["seq"], mesh.shape["head"]),
        mesh=mesh,
        in_specs=(P("seq", "head"), P("seq", "head"), P("seq", "head"), P(("seq", "head"), None)),
        out_specs=(P("seq", "head"), P("seq", "head"), P("seq", "head")),
        check_vma=False,
    )
```
